256 devices in a mesh: head: 4 (over z_hi), ctx: 64 (over x, y, z_lo, core).
Axes of the slice: x: 4, y: 4, z: 8 (z_hi: 4, z_lo: 2; z = z_hi * 2 + z_lo), core: 2. Of those that a mesh axis runs over, the one named last changes fastest.
Arguments:
- queries: bfloat16 [16384, 3584], P(('head', 'ctx')), may hold values from -6 to 6
- keys: bfloat16 [16384, 512], P(('head', 'ctx')), may hold values from -12 to 12
- values: bfloat16 [16384, 512], P(('head', 'ctx')), may hold values from -6 to 6
- block_index: int32 [128, 28, 128], replicated, may hold values from 0 to 127, as said below
- block_count: int32 [128, 28], replicated, may hold values from 1 to 128, as said below
- head_order: int32 [28], replicated, may hold values from 0 to 27, as said below
Outputs:
- attention_out: bfloat16 [16384, 3584], P(('head', 'ctx'))
The draws below stay inside these ranges and needn't reach their ends.
Inputs may be any that keep to these rules, and one draw needn't show every extreme that they name: For query block b and head h the first block_count[b, h] entries of block_index[b, h] are distinct key blocks in ascending order, always including block 0 and block b and never above b; the later entries name the remaining blocks. block_count[b, h] is at most b + 1. `head_order`: A permutation of the 28 query heads; each aligned block of 7 entries that starts at a multiple of 7 holds heads of exactly two key and value heads (head // 7).
All inputs are finite; a program needn't handle non-finite values.
Results may differ from the reference program's by a relative error of at most 0.0045.
Values may be sent and summed in bfloat16 or wider, within the bound.
No kernel may reach another device: no remote copies, remote signals or barrier semaphores. Data moves between devices by JAX's collectives and lax.ppermute only.
A program may use at most 64 MiB of HBM per device.

```python
import math
import jax
import jax.numpy as jnp
from jax import lax

H = 28
KVH = 4
HD = 128
BLOCK = 128
SEQ = 16384


def head_plan(key):
    per_group = H // KVH
    half_count = KVH // 2
    kv_order = jax.random.permutation(jax.random.fold_in(key, 101), KVH).astype(jnp.int32)
    head_iota = jnp.arange(H, dtype=jnp.int32)
    kv_of = head_iota // per_group
    is_dense = jnp.any(kv_of[:, None] == kv_order[None, :half_count], axis=1)
    strong = jax.random.randint(jax.random.fold_in(key, 102), (H,), 384, 1025)
    sparse = jax.random.randint(jax.random.fold_in(key, 103), (H,), 8, 97)
    chosen = jax.random.randint(jax.random.fold_in(key, 104), (KVH,), 0, per_group)
    full_head = head_iota % per_group == jnp.take(chosen, kv_of)
    limits = jnp.where(is_dense, jnp.where(full_head, 1024, strong), sparse)
    return (kv_order, limits)


def block_plan(key):
    kv_order, limits = head_plan(key)
    blocks = SEQ // BLOCK
    rolled = jax.random.randint(jax.random.fold_in(key, 105), (blocks, H, blocks), 0, 1024)
    query_block = jnp.arange(blocks, dtype=jnp.int32)[:, None, None]
    key_block = jnp.arange(blocks, dtype=jnp.int32)[None, None, :]
    attended = ((rolled < limits[None, :, None]) | (key_block == 0) | (key_block == query_block)) & (key_block <= query_block)
    ranking = jnp.where(attended, key_block, key_block + blocks)
    index_table = jnp.argsort(ranking, axis=-1, stable=True).astype(jnp.int32)
    count_table = jnp.sum(attended.astype(jnp.int32), axis=-1).astype(jnp.int32)
    return (index_table, count_table)


def draw_block_index(key, part):
    index_table, count_table = block_plan(key)
    return index_table


def draw_block_count(key, part):
    index_table, count_table = block_plan(key)
    return count_table


def draw_head_order(key, part):
    kv_order, limits = head_plan(key)
    key = jax.random.fold_in(key, 3)
    per_group = H // KVH
    half_count = KVH // 2
    lane_iota = jnp.arange(per_group, dtype=jnp.int32)
    split_at = jax.random.randint(jax.random.fold_in(key, 1), (half_count,), per_group // 2, per_group // 2 + 2)
    head_lists = []
    for pair_index in range(half_count):
        dense_kv = kv_order[pair_index]
        sparse_kv = kv_order[pair_index + half_count]
        dense_perm = jax.random.permutation(jax.random.fold_in(key, 10 + pair_index), per_group).astype(jnp.int32)
        sparse_perm = jax.random.permutation(jax.random.fold_in(key, 20 + pair_index), per_group).astype(jnp.int32)
        leading = lane_iota < split_at[pair_index]
        list_one = jnp.where(leading, dense_kv * per_group + dense_perm, sparse_kv * per_group + sparse_perm)
        list_two = jnp.where(leading, sparse_kv * per_group + sparse_perm, dense_kv * per_group + dense_perm)
        head_lists.append(list_one)
        head_lists.append(list_two)
    stacked = jnp.stack(head_lists)
    placing = jax.random.permutation(jax.random.fold_in(key, 30), KVH)
    return stacked[placing].reshape(H).astype(jnp.int32)


def draw_queries(key, part):
    key = jax.random.fold_in(key, 4)
    drawn = jnp.clip(jax.random.normal(key, (SEQ, H * HD), jnp.float32), -6.0, 6.0)
    return drawn.astype(jnp.bfloat16)


def draw_keys(key, part):
    key = jax.random.fold_in(key, 5)
    row_scales = jnp.exp(jax.random.uniform(jax.random.fold_in(key, 1), (SEQ, KVH, 1), jnp.float32, math.log(0.3), math.log(3.0)))
    drawn = jnp.clip(jax.random.normal(key, (SEQ, KVH, HD), jnp.float32), -4.0, 4.0) * row_scales
    return drawn.reshape(SEQ, KVH * HD).astype(jnp.bfloat16)


def block_scale(stream_key, shape, split, smallest, largest):
    def one(dim, parts):
        steps = jax.random.uniform(jax.random.fold_in(jax.random.fold_in(stream_key, 6), dim), (parts,), jnp.float32, smallest / len(split), largest / len(split))
        return jnp.repeat(jnp.exp(steps), shape[dim] // parts).reshape((-1,) + (1,) * (len(shape) - dim - 1))

    factor_of = one(*split[0])
    for cut in split[1:]:
        factor_of = factor_of * one(*cut)
    return factor_of


def normal_values(own_key, extent, scale, most, split=(), kind=jnp.bfloat16):
    result = jax.random.normal(own_key, extent, jnp.float32) * scale
    if len(split) > 0:
        result = block_scale(own_key, extent, split, -0.22, 0.18) * result
    return jnp.clip(result, min=-most, max=most).astype(kind)


def setup_inputs(seed: int = 0) -> dict:
    arg_keys = jax.random.split(jax.random.key(seed), 7)
    return {
        "queries": draw_queries(jax.random.fold_in(arg_keys[6], 71), 0),
        "keys": draw_keys(jax.random.fold_in(arg_keys[6], 71), 0),
        "values": normal_values(arg_keys[2], (SEQ, KVH * HD), 1.0, 6.0, ((0, 256),)),
        "block_index": draw_block_index(jax.random.fold_in(arg_keys[6], 71), 0),
        "block_count": draw_block_count(jax.random.fold_in(arg_keys[6], 71), 0),
        "head_order": draw_head_order(jax.random.fold_in(arg_keys[6], 71), 0),
    }


def attend_group(operands):
    query_tile, key_rows, value_rows, allowed = operands
    scores = jnp.einsum('gqd,kd->gqk', query_tile.astype(jnp.float32), key_rows.astype(jnp.float32)) * (1.0 / math.sqrt(HD))
    scores = jnp.where(allowed, scores, -jnp.inf)
    row_top = lax.optimization_barrier(jnp.max(scores, axis=-1, keepdims=True))
    weights = jnp.exp(scores - row_top)
    row_total = lax.optimization_barrier(jnp.sum(weights, axis=-1, keepdims=True))
    rounded = weights.astype(jnp.bfloat16)
    mixed_out = jnp.einsum('gqk,kd->gqd', rounded.astype(jnp.float32), value_rows.astype(jnp.float32))
    return mixed_out / row_total

def reference(queries, keys, values, block_index, block_count, head_order):
    per_group = H // KVH
    tile_rows = min(512, SEQ)
    per_tile = tile_rows // BLOCK
    blocks = SEQ // BLOCK
    query_heads = queries.reshape(SEQ, KVH, per_group, HD).transpose(1, 2, 0, 3)
    key_heads = keys.reshape(SEQ, KVH, HD).transpose(1, 0, 2)
    value_heads = values.reshape(SEQ, KVH, HD).transpose(1, 0, 2)
    block_iota = jnp.arange(blocks, dtype=jnp.int32)
    outputs = []
    for number in range(SEQ // tile_rows):
        length = (number + 1) * tile_rows
        first_row = number * tile_rows
        reach = length // BLOCK
        listed = block_index[number * per_tile:(number + 1) * per_tile]
        counted = block_count[number * per_tile:(number + 1) * per_tile]
        usable = block_iota[None, None, :] < counted[:, :, None]
        block_hits = (listed[:, :, :, None] == block_iota[None, None, None, :]) & usable[:, :, :, None]
        table_flags = jnp.any(block_hits, axis=2)[:, :, :reach]
        table_flags = table_flags.transpose(1, 0, 2).reshape(KVH, per_group, per_tile, 1, reach, 1)
        allowed = jnp.broadcast_to(table_flags, (KVH, per_group, per_tile, BLOCK, reach, BLOCK))
        allowed = allowed.reshape(KVH, per_group, tile_rows, length)
        query_pos = first_row + jnp.arange(tile_rows, dtype=jnp.int32)
        key_pos = jnp.arange(length, dtype=jnp.int32)
        allowed = allowed & (key_pos[None, :] <= query_pos[:, None])[None, None]
        mixed_out = lax.map(attend_group, (query_heads[:, :, first_row:first_row + tile_rows], key_heads[:, :length], value_heads[:, :length], allowed))
        outputs.append(mixed_out)
    attended = jnp.concatenate(outputs, axis=2).reshape(H, SEQ, HD)
    ordered = jnp.take(attended, head_order, axis=0)
    return ordered.transpose(1, 0, 2).reshape(SEQ, H * HD).astype(jnp.bfloat16)
```

```python
import math

import jax
import jax.numpy as jnp
from jax import lax
from jax.experimental import pallas as pl
from jax.experimental.pallas import tpu as pltpu
from jax.sharding import Mesh, PartitionSpec as P

H = 28
KVH = 4
HD = 128
BLOCK = 128
GROUP = H // KVH
TILES = 4 * GROUP
NB = 8
FLOOR = -1e30
EXP_SCALE = math.log2(math.e) / math.sqrt(HD)
AXES = ("zhi", "x", "y", "zlo", "core")
SHIFTS = (1, 3, 2)


def shift(array, axis, by):
    return lax.ppermute(array, axis, [(i, (i + by) % 4) for i in range(4)])


def swap_cores(array):
    return lax.ppermute(array, "core", [(0, 1), (1, 0)])


def tree(op, parts):
    while len(parts) > 1:
        parts = [op(*parts[i:i + 2]) if i + 1 < len(parts) else parts[i] for i in range(0, len(parts), 2)]
    return parts[0]


def attend_kernel(
    tab, cnt, q_own, q_oth, r0, r1, r2, r3, c0, c1, c2, c3, o_own, o_oth,
    kv, qt, s0, s1, s2, s3, p0, p1, m0, m1, m2, m3, a0, a1, a2, a3,
    m_ref, l_ref, acc, m_all, l_all, sem,
):
    s_bufs, p_bufs = (s0, s1, s2, s3), (p0, p1)
    m_bufs, a_bufs = (m0, m1, m2, m3), (a0, a1, a2, a3)
    here_x = lax.axis_index("x")
    here_y = lax.axis_index("y")
    core = lax.axis_index("core")
    offsets = (0,) + tuple(4 - s for s in SHIFTS)
    copies = []
    for a, by in enumerate(offsets):
        for b, across in enumerate(offsets):
            row_x = lax.rem(here_x + across, 4)
            row_y = lax.rem(here_y + by, 4)
            base = row_x * 32 + row_y * 8
            copies.append(((r0, r1, r2, r3)[a].at[b], kv.at[pl.ds(base, 4)]))
            col_y = lax.rem(here_y + across, 4)
            col_x = lax.rem(here_x + by, 4)
            base = col_x * 32 + col_y * 8 + 4
            copies.append(((c0, c1, c2, c3)[a].at[b], kv.at[pl.ds(base, 4)]))
    started = [pltpu.make_async_copy(src, dst, sem) for src, dst in copies]
    for copy in started:
        copy.start()

    def chunks_of(t):
        return (cnt[t] + (NB - 1)) // NB

    total = lax.fori_loop(0, TILES, lambda t, n: n + chunks_of(t), jnp.int32(0))
    keys = lax.broadcasted_iota(jnp.int32, (64, BLOCK), 0)
    rows = lax.broadcasted_iota(jnp.int32, (64, BLOCK), 1)
    seen = (keys <= rows) & (rows < 64) | (rows >= 64) & (core == 0)

    def start(t, _):
        q = jnp.concatenate([q_own[t], q_oth[t]], axis=0)
        qt[t] = q.T
        m_ref[t] = jnp.full((8, BLOCK), FLOOR, jnp.float32)
        l_ref[t] = jnp.zeros((8, BLOCK), jnp.float32)
        acc[t] = jnp.zeros((HD, BLOCK), jnp.float32)
        return 0

    lax.fori_loop(0, TILES, start, 0, unroll=2)
    m_ref[TILES] = jnp.zeros((8, BLOCK), jnp.float32)
    l_ref[TILES] = jnp.zeros((8, BLOCK), jnp.float32)
    acc[TILES] = jnp.zeros((HD, BLOCK), jnp.float32)
    for copy in started:
        copy.wait()

    def products(t, c, s_ref):
        k = jnp.concatenate([kv[tab[t, c * NB + j], 0] for j in range(NB)], axis=0)
        s = jnp.dot(k, qt[jnp.minimum(t, TILES - 1)], preferred_element_type=jnp.float32)
        left_over = cnt[t] - c * NB
        for j in range(NB):
            part = s[j * 64:(j + 1) * 64]
            s_ref[j * 64:(j + 1) * 64] = part if j == 0 else jnp.where(left_over > j, part, FLOOR)
        d = jnp.minimum(left_over, NB) - 1
        here = pl.ds(pl.multiple_of(d * 64, 64), 64)
        s_ref[here, :] = jnp.where(seen | (left_over > NB), s_ref[here, :], FLOOR)

    def tops(t, s_ref, m_buf, a_buf):
        top = tree(jnp.maximum, [s_ref[j * 64:(j + 1) * 64] for j in range(NB)])
        top = tree(jnp.maximum, [top[i * 8:(i + 1) * 8] for i in range(8)])
        m_old = m_ref[t]
        m_new = jnp.maximum(m_old, jnp.max(top, axis=0, keepdims=True))
        m_ref[t] = m_new
        m_buf[...] = m_new
        a_buf[...] = jnp.exp2((m_old - m_new) * EXP_SCALE)

    def weigh(t, s_ref, m_buf, a_buf, p_ref):
        m = m_buf[...][None]
        parts = []
        for j in range(NB):
            s = s_ref[j * 64:(j + 1) * 64].reshape(8, 8, BLOCK)
            p = jnp.exp2((s - m) * EXP_SCALE).reshape(64, BLOCK)
            p_ref[j * 64:(j + 1) * 64] = p.astype(jnp.bfloat16)
            parts.append(p)
        part = tree(jnp.add, parts)
        part = tree(jnp.add, [part[i * 8:(i + 1) * 8] for i in range(8)])
        l_ref[t] = l_ref[t] * a_buf[...] + part

    def mix(t, c, p_ref, a_buf):
        v = jnp.concatenate([kv[tab[t, c * NB + j], 1] for j in range(NB)], axis=0)
        update = lax.dot_general(v, p_ref[...], (((0,), (0,)), ((), ())), preferred_element_type=jnp.float32)
        acc[t] = acc[t] * a_buf[:1] + update

    def steps(_, carry):
        items = list(carry)
        for k in range(4):
            t, c = items[0], items[1]
            products(t, c, s_bufs[k])
            mix(items[6], items[7], p_bufs[(k + 1) % 2], a_bufs[(k + 1) % 4])
            tops(items[2], s_bufs[(k + 3) % 4], m_bufs[(k + 3) % 4], a_bufs[(k + 3) % 4])
            weigh(items[4], s_bufs[(k + 2) % 4], m_bufs[(k + 2) % 4], a_bufs[(k + 2) % 4], p_bufs[k % 2])
            last = c + 1 >= chunks_of(t)
            items = [jnp.where(last, jnp.minimum(t + 1, TILES), t), jnp.where(last, 0, c + 1)] + items[:6]
        return tuple(items)

    zero, dummy = jnp.int32(0), jnp.int32(TILES)
    lax.fori_loop(0, (total + 6) // 4, steps, (zero, zero, dummy, zero, dummy, zero, dummy, zero))

    def finish(t, _):
        o = acc[t].T
        o_own[t] = o[:64]
        o_oth[t] = o[64:]
        m_all[pl.ds(t, 1), :] = m_ref[t][:1]
        l_all[pl.ds(t, 1), :] = jnp.sum(l_ref[t], axis=0, keepdims=True)
        return 0

    m_all[...] = jnp.zeros_like(m_all)
    l_all[...] = jnp.zeros_like(l_all)
    lax.fori_loop(0, TILES, finish, 0, unroll=2)
    m = m_all[...].T
    l = l_all[...].T
    o_own[TILES] = m[:64]
    o_own[TILES + 1] = l[:64]
    o_oth[TILES] = m[64:]
    o_oth[TILES + 1] = l[64:]


def attend(tab, cnt, q_own, q_oth, rows, columns):
    vmem = pl.BlockSpec(memory_space=pltpu.VMEM)
    smem = pl.BlockSpec(memory_space=pltpu.SMEM)
    part = jax.ShapeDtypeStruct((TILES + 2, 64, HD), jnp.float32)
    return pl.pallas_call(
        attend_kernel,
        out_shape=(part, part),
        in_specs=[smem, smem, vmem, vmem] + [pl.BlockSpec(memory_space=pl.ANY)] * 8,
        out_specs=(vmem, vmem),
        scratch_shapes=[
            pltpu.VMEM((128, 2, 64, HD), jnp.bfloat16),
            pltpu.VMEM((TILES, HD, BLOCK), jnp.bfloat16),
        ]
        + [pltpu.VMEM((NB * 64, BLOCK), jnp.float32)] * 4
        + [pltpu.VMEM((NB * 64, BLOCK), jnp.bfloat16)] * 2
        + [pltpu.VMEM((8, BLOCK), jnp.float32)] * 8
        + [
            pltpu.VMEM((TILES + 1, 8, BLOCK), jnp.float32),
            pltpu.VMEM((TILES + 1, 8, BLOCK), jnp.float32),
            pltpu.VMEM((TILES + 1, HD, BLOCK), jnp.float32),
            pltpu.VMEM((BLOCK, BLOCK), jnp.float32),
            pltpu.VMEM((BLOCK, BLOCK), jnp.float32),
            pltpu.SemaphoreType.DMA,
        ],
        compiler_params=pltpu.CompilerParams(vmem_limit_bytes=40 * 2**20),
        name="attend",
    )(tab, cnt, q_own, q_oth, *rows, *columns)


def merge_kernel(a, b, out):
    m_a, m_b = a[TILES], b[TILES]
    top = jnp.maximum(m_a, m_b)
    w_a = jnp.exp2((m_a - top) * EXP_SCALE)
    w_b = jnp.exp2((m_b - top) * EXP_SCALE)
    whole = a[TILES + 1] * w_a + b[TILES + 1] * w_b
    lane = lax.broadcasted_iota(jnp.int32, (64, HD), 1)
    whole = jnp.where(lane < TILES, whole, 1.0)
    w_a, w_b = w_a / whole, w_b / whole
    for t in range(TILES):
        out[t] = (a[t] * w_a[:, t:t + 1] + b[t] * w_b[:, t:t + 1]).astype(jnp.bfloat16)


def merge(a, b):
    vmem = pl.BlockSpec(memory_space=pltpu.VMEM)
    return pl.pallas_call(
        merge_kernel,
        out_shape=jax.ShapeDtypeStruct((TILES, 64, HD), jnp.bfloat16),
        in_specs=[vmem, vmem],
        out_specs=vmem,
        name="merge",
    )(a, b)


def place_kernel(order, heads, out):
    for j in range(H):
        out[:, j * HD:(j + 1) * HD] = heads[order[j]]


def place(order, heads):
    return pl.pallas_call(
        place_kernel,
        out_shape=jax.ShapeDtypeStruct((64, H * HD), jnp.bfloat16),
        in_specs=[
            pl.BlockSpec(memory_space=pltpu.SMEM),
            pl.BlockSpec(memory_space=pltpu.VMEM),
        ],
        out_specs=pl.BlockSpec(memory_space=pltpu.VMEM),
        name="place",
    )(order, heads)


def split_kernel(queries, keys, values, q_out, kv_out):
    for h in range(H):
        q_out[h] = queries[:, h * HD:(h + 1) * HD]
    for g in range(KVH):
        for copy in range(2):
            kv_out[2 * g + copy, 0] = keys[:, g * HD:(g + 1) * HD]
            kv_out[2 * g + copy, 1] = values[:, g * HD:(g + 1) * HD]


def split(queries, keys, values):
    vmem = pl.BlockSpec(memory_space=pltpu.VMEM)
    return pl.pallas_call(
        split_kernel,
        out_shape=(
            jax.ShapeDtypeStruct((H, 64, HD), jnp.bfloat16),
            jax.ShapeDtypeStruct((8, 2, 64, HD), jnp.bfloat16),
        ),
        in_specs=[vmem, vmem, vmem],
        out_specs=(vmem, vmem),
        name="split",
    )(queries, keys, values)


def tables(block_index, block_count):
    chip = (lax.axis_index("x") * 4 + lax.axis_index("y")) * 2 + lax.axis_index("zlo")
    group = lax.axis_index("zhi")
    index = block_index.reshape(4, 32, KVH, GROUP, 128)
    index = lax.dynamic_slice(index, (0, chip, group, 0, 0), (4, 1, 1, GROUP, 128))
    index = index.reshape(TILES, 128)
    count = block_count.reshape(4, 32, KVH, GROUP)
    count = lax.dynamic_slice(count, (0, chip, group, 0), (4, 1, 1, GROUP)).reshape(TILES)
    inner = index % 32
    slots = (inner // 2) * 8 + (index // 32) * 2 + inner % 2
    slots = jnp.pad(slots, ((0, 1), (0, 0)))
    return slots, jnp.pad(count, (0, 1), constant_values=1)


def local(queries, keys, values, block_index, block_count, head_order):
    q_sent, kv_sent = split(queries, keys, values)
    kv_got = lax.all_to_all(kv_sent, ("zhi", "zlo"), split_axis=0, concat_axis=0, tiled=True)
    q_own = lax.all_to_all(
        q_sent.reshape(4, GROUP * 64, HD), "zhi", split_axis=0, concat_axis=0, tiled=True
    ).reshape(TILES, 64, HD)
    q_oth = swap_cores(q_own)
    low, high = kv_got[:4], kv_got[4:]
    near = lax.optimization_barrier(
        [shift(low, "x", s) for s in SHIFTS] + [shift(high, "y", s) for s in SHIFTS]
    )
    row = jnp.stack([low] + near[:3])
    column = jnp.stack([high] + near[3:])
    rows = [row] + [shift(row, "y", s) for s in SHIFTS]
    columns = [column] + [shift(column, "x", s) for s in SHIFTS]
    slots, count = tables(block_index, block_count)
    mine, others = attend(slots, count, q_own, q_oth, rows, columns)
    attended = merge(mine, swap_cores(others))
    returned = lax.all_to_all(
        attended.reshape(4, GROUP * 64, HD), "zhi", split_axis=0, concat_axis=0, tiled=True
    ).reshape(H, 64, HD)
    return place(head_order, returned)


def solution(mesh):
    wide = Mesh(mesh.devices.reshape(4, 4, 4, 2, 2), AXES)
    tokens = P(AXES, None)
    return jax.shard_map(
        local,
        mesh=wide,
        in_specs=(tokens, tokens, tokens, P(), P(), P()),
        out_specs=tokens,
        check_vma=False,
    )
```

```python
import math
from functools import partial

import jax
import jax.numpy as jnp
from jax import lax
from jax.experimental import pallas as pl
from jax.experimental.pallas import tpu as pltpu
from jax.sharding import Mesh, PartitionSpec as P

H = 28
KVH = 4
HD = 128
BLOCK = 128
GROUP = H // KVH
TILES = 4 * GROUP
NB = 8
FLOOR = -1e30
EXP_SCALE = math.log2(math.e) / math.sqrt(HD)
AXES = ("zhi", "x", "y", "zlo", "core")


def partner(array, axis, mask):
    return lax.ppermute(array, axis, [(i, i ^ mask) for i in range(lax.axis_size(axis))])


def swap_cores(array):
    return partner(array, "core", 1)


def tree(op, parts):
    while len(parts) > 1:
        parts = [op(*parts[i:i + 2]) if i + 1 < len(parts) else parts[i] for i in range(0, len(parts), 2)]
    return parts[0]


def attend_kernel(first, pieces, *refs):
    refs = list(refs)
    take = lambda n: [refs.pop(0) for _ in range(n)]
    tab, cnt = take(2)
    queries = take(2) if first else take(1)
    sources = take(pieces)
    state_in = [] if first else take(3)
    outs = take(4) if first else take(2)
    (kv,) = take(1)
    s_bufs, m_bufs, a_bufs = take(4), take(4), take(4)
    m_ref, l_ref, acc = outs[:3] if first else take(3)
    qt = outs[3] if first else queries[0]
    lse = None if first else take(1)[0]
    (sem,) = refs
    core = lax.axis_index("core")
    started, at = [], 0
    for source in sources:
        started.append(pltpu.make_async_copy(source, kv.at[pl.ds(at, source.shape[0])], sem))
        at += source.shape[0]
    for copy in started:
        copy.start()

    def chunks_of(t):
        return jnp.maximum((cnt[t] + (NB - 1)) // NB, 1)

    total = lax.fori_loop(0, TILES, lambda t, n: n + chunks_of(t), jnp.int32(0))
    keys = lax.broadcasted_iota(jnp.int32, (64, BLOCK), 0)
    rows = lax.broadcasted_iota(jnp.int32, (64, BLOCK), 1)
    seen = (keys <= rows) & (rows < 64) | (rows >= 64) & (core == 0)

    def start(t, _):
        if first:
            qt[t] = jnp.concatenate([queries[0][t], queries[1][t]], axis=0).T
            m_ref[t] = jnp.full((8, BLOCK), FLOOR, jnp.float32)
            l_ref[t] = jnp.zeros((8, BLOCK), jnp.float32)
            acc[t] = jnp.zeros((HD, BLOCK), jnp.float32)
        else:
            m_ref[t], l_ref[t], acc[t] = (ref[t] for ref in state_in)
        return 0

    lax.fori_loop(0, TILES, start, 0, unroll=2)
    m_ref[TILES] = jnp.zeros((8, BLOCK), jnp.float32)
    l_ref[TILES] = jnp.zeros((8, BLOCK), jnp.float32)
    acc[TILES] = jnp.zeros((HD, BLOCK), jnp.float32)
    for copy in started:
        copy.wait()

    def block(t, c, j, which):
        return kv[tab[t, c * NB + j], which]

    def products(t, c, s_ref, m_buf, a_buf):
        k = jnp.concatenate([block(t, c, j, 0) for j in range(NB)], axis=0)
        s = jnp.dot(k, qt[jnp.minimum(t, TILES - 1)], preferred_element_type=jnp.float32)
        left_over = cnt[t] - c * NB
        d = jnp.minimum(left_over, NB) - 1
        tops = []
        for j in range(NB):
            part = s[j * 64:(j + 1) * 64]
            top = jnp.max(part.reshape(8, 8, BLOCK), axis=0)
            tops.append(jnp.where((left_over > j) & ((d != j) | (left_over > NB)) if first else left_over > j, top, FLOOR))
            s_ref[j * 64:(j + 1) * 64] = jnp.where(left_over > j, part, FLOOR)
        if first:
            here = pl.ds(pl.multiple_of(d * 64, 64), 64)
            part = jnp.where(seen | (left_over > NB), s_ref[here, :], FLOOR)
            s_ref[here, :] = part
            tops.append(jnp.max(part.reshape(8, 8, BLOCK), axis=0))
        m_old = m_ref[t]
        m_new = jnp.maximum(m_old, jnp.max(tree(jnp.maximum, tops), axis=0, keepdims=True))
        m_ref[t] = m_new
        m_buf[...] = m_new
        a_buf[...] = jnp.exp2((m_old - m_new) * EXP_SCALE)

    def weigh(t, c, s_ref, m_buf, a_buf):
        m = m_buf[...][None]
        parts = []
        for j in range(NB):
            s = s_ref[j * 64:(j + 1) * 64].reshape(8, 8, BLOCK)
            parts.append(jnp.exp2((s - m) * EXP_SCALE).reshape(64, BLOCK))
        p = jnp.concatenate([part.astype(jnp.bfloat16) for part in parts], axis=0)
        part = tree(jnp.add, parts)
        part = tree(jnp.add, [part[i * 8:(i + 1) * 8] for i in range(8)])
        l_ref[t] = l_ref[t] * a_buf[...] + part
        v = jnp.concatenate([block(t, c, j, 1) for j in range(NB)], axis=0)
        update = lax.dot_general(
            v, p, (((0,), (0,)), ((), ())), preferred_element_type=jnp.float32
        )
        acc[t] = acc[t] * a_buf[:1] + update

    def steps(_, carry):
        items = list(carry)
        for k in range(8):
            t, c = items[0], items[1]
            old = (k - 3) % 8
            products(t, c, s_bufs[k % 4], m_bufs[k % 4], a_bufs[k % 4])
            weigh(items[6], items[7], s_bufs[old % 4], m_bufs[old % 4], a_bufs[old % 4])
            last = c + 1 >= chunks_of(t)
            items = [
                jnp.where(last, jnp.minimum(t + 1, TILES), t),
                jnp.where(last, 0, c + 1),
            ] + items[:6]
        return tuple(items)

    zero, dummy = jnp.int32(0), jnp.int32(TILES)
    lax.fori_loop(0, (total + 10) // 8, steps, (zero, zero) + (dummy, zero) * 3)
    if first:
        return
    o_own, o_oth = outs
    lse[...] = jnp.zeros_like(lse)

    def finish(t, _):
        whole = jnp.sum(l_ref[t], axis=0, keepdims=True)
        o = (acc[t] / whole).T.astype(jnp.bfloat16)
        o_own[t] = o[:64]
        o_oth[t] = o[64:]
        lse[pl.ds(t, 1), :] = m_ref[t][:1] * EXP_SCALE + jnp.log2(whole)
        return 0

    lax.fori_loop(0, TILES, finish, 0, unroll=2)
    rest = lse[...].T
    for i in range(3):
        part = rest.astype(jnp.bfloat16)
        o_own[TILES + i] = part[:64]
        o_oth[TILES + i] = part[64:]
        rest = rest - part.astype(jnp.float32)


def attend(tab, cnt, queries, pieces, state):
    vmem = pl.BlockSpec(memory_space=pltpu.VMEM)
    smem = pl.BlockSpec(memory_space=pltpu.SMEM)
    small = ((TILES + 1, 8, BLOCK), jnp.float32)
    large = ((TILES + 1, HD, BLOCK), jnp.float32)
    if state is None:
        shapes = [small, small, large, ((TILES, HD, BLOCK), jnp.bfloat16)]
        kept = []
    else:
        shapes = [((TILES + 3, 64, HD), jnp.bfloat16)] * 2
        kept = [pltpu.VMEM(*small), pltpu.VMEM(*small), pltpu.VMEM(*large)]
        kept += [pltpu.VMEM((BLOCK, BLOCK), jnp.float32)]
    slots = sum(piece.shape[0] for piece in pieces)
    flops = 2 * 2 * BLOCK * HD * 64 * TILES * slots // 2
    return pl.pallas_call(
        partial(attend_kernel, state is None, len(pieces)),
        out_shape=tuple(jax.ShapeDtypeStruct(*a) for a in shapes),
        in_specs=[smem, smem]
        + [vmem] * len(queries)
        + [pl.BlockSpec(memory_space=pl.ANY)] * len(pieces)
        + [vmem] * (0 if state is None else 3),
        out_specs=(vmem,) * len(shapes),
        scratch_shapes=[pltpu.VMEM((slots, 2, 64, HD), jnp.bfloat16)]
        + [pltpu.VMEM((NB * 64, BLOCK), jnp.float32)] * 4
        + [pltpu.VMEM((8, BLOCK), jnp.float32)] * 8
        + kept
        + [pltpu.SemaphoreType.DMA],
        compiler_params=pltpu.CompilerParams(vmem_limit_bytes=40 * 2**20),
        cost_estimate=pl.CostEstimate(
            flops=4 * flops, bytes_accessed=slots * 2**15, transcendentals=flops // 256
        ),
        name="attend",
    )(tab, cnt, *queries, *pieces, *(state or ()))


def merge_kernel(a, b, out):
    lse_a, lse_b = (
        sum(ref[TILES + i].astype(jnp.float32) for i in range(3)) for ref in (a, b)
    )
    top = jnp.maximum(lse_a, lse_b)
    w_a = jnp.exp2(lse_a - top)
    w_b = jnp.exp2(lse_b - top)
    w_a = w_a / (w_a + w_b)
    w_b = 1.0 - w_a
    for t in range(TILES):
        mixed = a[t].astype(jnp.float32) * w_a[:, t:t + 1]
        mixed = mixed + b[t].astype(jnp.float32) * w_b[:, t:t + 1]
        out[t] = mixed.astype(jnp.bfloat16)


def merge(a, b):
    vmem = pl.BlockSpec(memory_space=pltpu.VMEM)
    return pl.pallas_call(
        merge_kernel,
        out_shape=jax.ShapeDtypeStruct((TILES, 64, HD), jnp.bfloat16),
        in_specs=[vmem, vmem],
        out_specs=vmem,
        name="merge",
    )(a, b)


def place_kernel(order, heads, out):
    for j in range(H):
        out[:, j * HD:(j + 1) * HD] = heads[order[j]]


def place(order, heads):
    return pl.pallas_call(
        place_kernel,
        out_shape=jax.ShapeDtypeStruct((64, H * HD), jnp.bfloat16),
        in_specs=[
            pl.BlockSpec(memory_space=pltpu.SMEM),
            pl.BlockSpec(memory_space=pltpu.VMEM),
        ],
        out_specs=pl.BlockSpec(memory_space=pltpu.VMEM),
        name="place",
    )(order, heads)


def split_q_kernel(queries, out):
    for h in range(H):
        out[h] = queries[:, h * HD:(h + 1) * HD]


def split_kv_kernel(keys, values, out):
    for g in range(KVH):
        for copy in range(2):
            out[2 * g + copy, 0] = keys[:, g * HD:(g + 1) * HD]
            out[2 * g + copy, 1] = values[:, g * HD:(g + 1) * HD]


def split(kernel, shape, *arrays):
    vmem = pl.BlockSpec(memory_space=pltpu.VMEM)
    return pl.pallas_call(
        kernel,
        out_shape=jax.ShapeDtypeStruct(shape, jnp.bfloat16),
        in_specs=[vmem] * len(arrays),
        out_specs=vmem,
        name="split",
    )(*arrays)


def tables(block_index, block_count):
    here_x, here_y = lax.axis_index("x"), lax.axis_index("y")
    chip = (here_x * 4 + here_y) * 2 + lax.axis_index("zlo")
    group = lax.axis_index("zhi")
    index = block_index.reshape(4, 32, KVH, GROUP, 128)
    index = lax.dynamic_slice(index, (0, chip, group, 0, 0), (4, 1, 1, GROUP, 128))
    index = index.reshape(TILES, 128)
    count = block_count.reshape(4, 32, KVH, GROUP)
    count = lax.dynamic_slice(count, (0, chip, group, 0), (4, 1, 1, GROUP)).reshape(TILES, 1)

    z, inner = index // 32, index % 32
    rel_x, rel_y = (inner // 8) ^ here_x, (inner // 2 % 4) ^ here_y
    low = z < 2
    within, away = jnp.where(low, rel_x, rel_y), jnp.where(low, rel_y, rel_x)
    half = within // 2
    spot = jnp.where(half == 0, within, 3 - within) * 4 + z % 2 * 2 + inner % 2
    soon = away == jnp.where(half == 0, 1, 3)
    first = (away == 0) | soon
    slot_first = jnp.where(soon, 16, 0) + half * 8
    slot_second = half * 16 + jnp.where(away == 2, 8, 0)
    slot = jnp.where(first, slot_first, slot_second) + spot + jnp.where(low, 0, 32)
    entry = lax.broadcasted_iota(jnp.int32, (TILES, 128), 1)
    stage = jnp.where(entry < count, jnp.where(first, 0, 1), -1)
    before = lax.broadcasted_iota(jnp.int32, (128, 128), 0) <= lax.broadcasted_iota(
        jnp.int32, (128, 128), 1
    )
    result = []
    for number in range(2):
        member = stage == number
        rank = jnp.dot(
            member.astype(jnp.bfloat16), before.astype(jnp.bfloat16),
            preferred_element_type=jnp.float32,
        ).astype(jnp.int32)
        hit = (jnp.where(member, rank, 0)[:, :, None] - 1) == entry[:, None, :]
        packed = jnp.sum(jnp.where(hit, slot[:, :, None], 0), axis=1)
        packed = jnp.pad(packed, ((0, 1), (0, 0)))
        result.append((packed, jnp.pad(rank[:, 127], (0, 1), constant_values=1)))
    return result


def local(queries, keys, values, block_index, block_count, head_order):
    kv_sent = split(split_kv_kernel, (8, 2, 64, HD), keys, values)
    kv_got = lax.all_to_all(kv_sent, ("zhi", "zlo"), split_axis=0, concat_axis=0, tiled=True)
    low, high = kv_got[:4], kv_got[4:]
    low_next, high_next = partner(low, "x", 1), partner(high, "y", 1)
    q_sent = split(split_q_kernel, (H, 64, HD), queries)
    q_own = lax.all_to_all(
        q_sent.reshape(4, GROUP * 64, HD), "zhi", split_axis=0, concat_axis=0, tiled=True
    ).reshape(TILES, 64, HD)
    q_oth = swap_cores(q_own)
    early, late = [], []
    for mine, other, inner, outer in ((low, low_next, "x", "y"), (high, high_next, "y", "x")):
        one = jnp.concatenate([mine, other])
        two = partner(one, inner, 3)
        one_next, two_next = partner(one, outer, 1), partner(two, outer, 3)
        early += [one, two, one_next, two_next]
        late += [
            partner(jnp.concatenate([one, one_next]), outer, 3),
            partner(jnp.concatenate([two, two_next]), outer, 1),
        ]
    ready, arriving = tables(block_index, block_count)
    *state, turned = attend(*ready, [q_own, q_oth], early, None)
    mine, others = attend(*arriving, [turned], late, state)
    attended = merge(mine, swap_cores(others))
    returned = lax.all_to_all(
        attended.reshape(4, GROUP * 64, HD), "zhi", split_axis=0, concat_axis=0, tiled=True
    ).reshape(H, 64, HD)
    return place(head_order, returned)


def solution(mesh):
    wide = Mesh(mesh.devices.reshape(4, 4, 4, 2, 2), AXES)
    tokens = P(AXES, None)
    return jax.shard_map(
        local,
        mesh=wide,
        in_specs=(tokens, tokens, tokens, P(), P(), P()),
        out_specs=tokens,
        check_vma=False,
    )
```

```python
import math
from functools import partial

import jax
import jax.numpy as jnp
from jax import lax
from jax.experimental import pallas as pl
from jax.experimental.pallas import tpu as pltpu
from jax.sharding import Mesh, PartitionSpec as P

H = 28
KVH = 4
HD = 128
BLOCK = 128
GROUP = H // KVH
TILES = 4 * GROUP
NB = 8
FLOOR = -1e30
EXP_SCALE = math.log2(math.e) / math.sqrt(HD)
AXES = ("zhi", "x", "y", "zlo", "core")


def partner(array, axis, mask):
    return lax.ppermute(array, axis, [(i, i ^ mask) for i in range(lax.axis_size(axis))])


def swap_cores(array):
    return partner(array, "core", 1)


def tree(op, parts):
    while len(parts) > 1:
        parts = [op(*parts[i:i + 2]) if i + 1 < len(parts) else parts[i] for i in range(0, len(parts), 2)]
    return parts[0]


def attend_kernel(first, pieces, *refs):
    refs = list(refs)
    take = lambda n: [refs.pop(0) for _ in range(n)]
    tab, cnt = take(2)
    queries = take(2) if first else take(1)
    sources = take(pieces)
    state_in = [] if first else take(3)
    outs = take(4) if first else take(2)
    (kv,) = take(1)
    s_bufs, m_bufs, a_bufs = take(4), take(4), take(4)
    m_ref, l_ref, acc = outs[:3] if first else take(3)
    qt = outs[3] if first else queries[0]
    lse, whole_out = (None, None) if first else take(2)
    (sem,) = refs
    core = lax.axis_index("core")
    started, at = [], 0
    for source in sources:
        started.append(pltpu.make_async_copy(source, kv.at[pl.ds(at, source.shape[0])], sem))
        at += source.shape[0]
    for copy in started:
        copy.start()

    def chunks_of(t):
        return jnp.maximum((cnt[t] + (NB - 1)) // NB, 1)

    total = lax.fori_loop(0, TILES, lambda t, n: n + chunks_of(t), jnp.int32(0))
    keys = lax.broadcasted_iota(jnp.int32, (64, BLOCK), 0)
    rows = lax.broadcasted_iota(jnp.int32, (64, BLOCK), 1)
    seen = (keys <= rows) & (rows < 64) | (rows >= 64) & (core == 0)

    def start(t, _):
        if first:
            qt[t] = jnp.concatenate([queries[0][t], queries[1][t]], axis=0).T
            m_ref[t] = jnp.full((8, BLOCK), FLOOR, jnp.float32)
            l_ref[t] = jnp.zeros((8, BLOCK), jnp.float32)
            acc[t] = jnp.zeros((HD, BLOCK), jnp.float32)
        else:
            m_ref[t], l_ref[t], acc[t] = (ref[t] for ref in state_in)
        return 0

    lax.fori_loop(0, TILES, start, 0, unroll=2)
    m_ref[TILES] = jnp.zeros((8, BLOCK), jnp.float32)
    l_ref[TILES] = jnp.zeros((8, BLOCK), jnp.float32)
    acc[TILES] = jnp.zeros((HD, BLOCK), jnp.float32)
    for copy in started:
        copy.wait()

    def block(t, c, j, which):
        return kv[tab[t, c * NB + j], which]

    def products(t, c, s_ref, m_buf, a_buf):
        k = jnp.concatenate([block(t, c, j, 0) for j in range(NB)], axis=0)
        s = jnp.dot(k, qt[jnp.minimum(t, TILES - 1)], preferred_element_type=jnp.float32)
        left_over = cnt[t] - c * NB
        d = jnp.minimum(left_over, NB) - 1
        tops = []
        for j in range(NB):
            part = s[j * 64:(j + 1) * 64]
            top = jnp.max(part.reshape(8, 8, BLOCK), axis=0)
            tops.append(jnp.where((left_over > j) & ((d != j) | (left_over > NB)) if first else left_over > j, top, FLOOR))
            s_ref[j * 64:(j + 1) * 64] = jnp.where(left_over > j, part, FLOOR)
        if first:
            here = pl.ds(pl.multiple_of(d * 64, 64), 64)
            part = jnp.where(seen | (left_over > NB), s_ref[here, :], FLOOR)
            s_ref[here, :] = part
            tops.append(jnp.max(part.reshape(8, 8, BLOCK), axis=0))
        m_old = m_ref[t]
        m_new = jnp.maximum(m_old, jnp.max(tree(jnp.maximum, tops), axis=0, keepdims=True))
        m_ref[t] = m_new
        m_buf[...] = m_new
        a_buf[...] = jnp.exp2((m_old - m_new) * EXP_SCALE)

    def weigh(t, c, s_ref, m_buf, a_buf):
        m = m_buf[...][None]
        parts = []
        for j in range(NB):
            s = s_ref[j * 64:(j + 1) * 64].reshape(8, 8, BLOCK)
            parts.append(jnp.exp2((s - m) * EXP_SCALE).reshape(64, BLOCK))
        p = jnp.concatenate([part.astype(jnp.bfloat16) for part in parts], axis=0)
        part = tree(jnp.add, parts)
        part = tree(jnp.add, [part[i * 8:(i + 1) * 8] for i in range(8)])
        l_ref[t] = l_ref[t] * a_buf[...] + part
        v = jnp.concatenate([block(t, c, j, 1) for j in range(NB)], axis=0)
        update = lax.dot_general(
            v, p, (((0,), (0,)), ((), ())), preferred_element_type=jnp.float32
        )
        acc[t] = acc[t] * a_buf[:1] + update

    def steps(_, carry):
        items = list(carry)
        for k in range(8):
            t, c = items[0], items[1]
            old = (k - 3) % 8
            products(t, c, s_bufs[k % 4], m_bufs[k % 4], a_bufs[k % 4])
            weigh(items[6], items[7], s_bufs[old % 4], m_bufs[old % 4], a_bufs[old % 4])
            last = c + 1 >= chunks_of(t)
            items = [
                jnp.where(last, jnp.minimum(t + 1, TILES), t),
                jnp.where(last, 0, c + 1),
            ] + items[:6]
        return tuple(items)

    zero, dummy = jnp.int32(0), jnp.int32(TILES)
    lax.fori_loop(0, (total + 10) // 8, steps, (zero, zero) + (dummy, zero) * 3)
    if first:
        return
    lse[...] = jnp.zeros_like(lse)

    def finish(t, _):
        whole = jnp.sum(l_ref[t], axis=0, keepdims=True)
        whole_out[t] = (acc[t] / whole).T
        lse[pl.ds(t, 1), :] = m_ref[t][:1] * EXP_SCALE + jnp.log2(whole)
        return 0

    leaving = []

    def leave(at, count):
        for i, out in enumerate(outs):
            leaving.append(
                pltpu.make_async_copy(
                    whole_out.at[pl.ds(at, count), pl.ds(i * 64, 64)],
                    out.at[pl.ds(at, count)],
                    sem,
                )
            )
            leaving[-1].start()

    for stripe in range(4):
        lax.fori_loop(stripe * GROUP, (stripe + 1) * GROUP, finish, 0, unroll=GROUP)
        leave(stripe * GROUP, GROUP)
    whole_out[TILES] = lse[...].T
    leave(TILES, 1)
    for copy in leaving:
        copy.wait()


def attend(tab, cnt, queries, pieces, state):
    vmem = pl.BlockSpec(memory_space=pltpu.VMEM)
    smem = pl.BlockSpec(memory_space=pltpu.SMEM)
    small = ((TILES + 1, 8, BLOCK), jnp.float32)
    large = ((TILES + 1, HD, BLOCK), jnp.float32)
    if state is None:
        shapes = [small, small, large, ((TILES, HD, BLOCK), jnp.bfloat16)]
        kept = []
    else:
        shapes = [((TILES + 1, 64, HD), jnp.float32)] * 2
        kept = [pltpu.VMEM(*small), pltpu.VMEM(*small), pltpu.VMEM(*large)]
        kept += [pltpu.VMEM((BLOCK, BLOCK), jnp.float32), pltpu.VMEM(*large)]
    slots = sum(piece.shape[0] for piece in pieces)
    flops = 2 * 2 * BLOCK * HD * 64 * TILES * slots // 2
    return pl.pallas_call(
        partial(attend_kernel, state is None, len(pieces)),
        out_shape=tuple(jax.ShapeDtypeStruct(*a) for a in shapes),
        in_specs=[smem, smem]
        + [vmem] * len(queries)
        + [pl.BlockSpec(memory_space=pl.ANY)] * len(pieces)
        + [vmem] * (0 if state is None else 3),
        out_specs=(vmem if state is None else pl.BlockSpec(memory_space=pltpu.HBM),) * len(shapes),
        scratch_shapes=[pltpu.VMEM((slots, 2, 64, HD), jnp.bfloat16)]
        + [pltpu.VMEM((NB * 64, BLOCK), jnp.float32)] * 4
        + [pltpu.VMEM((8, BLOCK), jnp.float32)] * 8
        + kept
        + [pltpu.SemaphoreType.DMA],
        compiler_params=pltpu.CompilerParams(vmem_limit_bytes=40 * 2**20),
        cost_estimate=pl.CostEstimate(
            flops=4 * flops, bytes_accessed=slots * 2**15, transcendentals=flops // 256
        ),
        name="attend",
    )(tab, cnt, *queries, *pieces, *(state or ()))


def merge_kernel(a_far, b_far, out_far, a, b, out, sems):
    spans = [(TILES, 1)] + [(i * GROUP, GROUP) for i in range(4)]
    arriving = [
        [
            pltpu.make_async_copy(
                far.at[pl.ds(at, count)], near.at[pl.ds(at, count)], sems.at[2 * i + k]
            )
            for k, (far, near) in enumerate(((a_far, a), (b_far, b)))
        ]
        for i, (at, count) in enumerate(spans)
    ]
    for copies in arriving:
        for copy in copies:
            copy.start()
    leaving = []
    for i, (at, count) in enumerate(spans):
        for copy in arriving[i]:
            copy.wait()
        if i == 0:
            top = jnp.maximum(a[TILES], b[TILES])
            w_a = jnp.exp2(a[TILES] - top)
            w_b = jnp.exp2(b[TILES] - top)
            w_a = w_a / (w_a + w_b)
            w_b = 1.0 - w_a
            continue
        for t in range(at, at + count):
            out[t] = (a[t] * w_a[:, t:t + 1] + b[t] * w_b[:, t:t + 1]).astype(jnp.bfloat16)
        leaving.append(
            pltpu.make_async_copy(
                out.at[pl.ds(at, count)], out_far.at[pl.ds(at, count)], sems.at[9 + i]
            )
        )
        leaving[-1].start()
    for copy in leaving:
        copy.wait()


def merge(a, b):
    far = pl.BlockSpec(memory_space=pltpu.HBM)
    part = pltpu.VMEM((TILES + 1, 64, HD), jnp.float32)
    return pl.pallas_call(
        merge_kernel,
        out_shape=jax.ShapeDtypeStruct((TILES, 64, HD), jnp.bfloat16),
        in_specs=[far, far],
        out_specs=far,
        scratch_shapes=[
            part, part, pltpu.VMEM((TILES, 64, HD), jnp.bfloat16), pltpu.SemaphoreType.DMA((14,))
        ],
        name="merge",
    )(a, b)


def place_kernel(spot, heads, out):
    for h in range(H):
        at = pl.multiple_of(spot[h] * HD, HD)
        out[:, pl.ds(at, HD)] = heads[h]


def place(order, heads):
    heads_iota = jnp.arange(H, dtype=jnp.int32)
    spot = jnp.sum(jnp.where(order[:, None] == heads_iota[None], heads_iota[:, None], 0), axis=0)
    return pl.pallas_call(
        place_kernel,
        out_shape=jax.ShapeDtypeStruct((64, H * HD), jnp.bfloat16),
        in_specs=[
            pl.BlockSpec(memory_space=pltpu.SMEM),
            pl.BlockSpec(memory_space=pltpu.VMEM),
        ],
        out_specs=pl.BlockSpec(memory_space=pltpu.VMEM),
        name="place",
    )(spot, heads)


def split_q_kernel(queries, out):
    for h in range(H):
        out[h] = queries[:, h * HD:(h + 1) * HD]


def split_kv_kernel(keys, values, out):
    for g in range(KVH):
        for copy in range(2):
            out[2 * g + copy, 0] = keys[:, g * HD:(g + 1) * HD]
            out[2 * g + copy, 1] = values[:, g * HD:(g + 1) * HD]


def split(kernel, shapes, *arrays):
    vmem = pl.BlockSpec(memory_space=pltpu.VMEM)
    return pl.pallas_call(
        kernel,
        out_shape=tuple(jax.ShapeDtypeStruct(shape, jnp.bfloat16) for shape in shapes),
        in_specs=[vmem] * len(arrays),
        out_specs=(vmem,) * len(shapes),
        name="split",
    )(*arrays)


def tables(block_index, block_count):
    here_x, here_y = lax.axis_index("x"), lax.axis_index("y")
    chip = (here_x * 4 + here_y) * 2 + lax.axis_index("zlo")
    group = lax.axis_index("zhi")
    index = block_index.reshape(4, 32, KVH, GROUP, 128)
    index = lax.dynamic_slice(index, (0, chip, group, 0, 0), (4, 1, 1, GROUP, 128))
    index = index.reshape(TILES, 128)
    count = block_count.reshape(4, 32, KVH, GROUP)
    count = lax.dynamic_slice(count, (0, chip, group, 0), (4, 1, 1, GROUP)).reshape(TILES, 1)

    z, inner = index // 32, index % 32
    rel_x, rel_y = (inner // 8) ^ here_x, (inner // 2 % 4) ^ here_y
    low = z < 2
    within, away = jnp.where(low, rel_x, rel_y), jnp.where(low, rel_y, rel_x)
    half = within // 2
    spot = jnp.where(half == 0, within, 3 - within) * 4 + z % 2 * 2 + inner % 2
    soon = away == jnp.where(half == 0, 1, 3)
    first = (away == 0) | soon
    slot_first = jnp.where(soon, 16, 0) + half * 8
    slot_second = half * 16 + jnp.where(away == 2, 8, 0)
    slot = jnp.where(first, slot_first, slot_second) + spot + jnp.where(low, 0, 32)
    entry = lax.broadcasted_iota(jnp.int32, (TILES, 128), 1)
    stage = jnp.where(entry < count, jnp.where(first, 0, 1), -1)
    before = lax.broadcasted_iota(jnp.int32, (128, 128), 0) <= lax.broadcasted_iota(
        jnp.int32, (128, 128), 1
    )
    result = []
    for number in range(2):
        member = stage == number
        rank = jnp.dot(
            member.astype(jnp.bfloat16), before.astype(jnp.bfloat16),
            preferred_element_type=jnp.float32,
        ).astype(jnp.int32)
        hit = (jnp.where(member, rank, 0)[:, :, None] - 1) == entry[:, None, :]
        packed = jnp.sum(jnp.where(hit, slot[:, :, None], 0), axis=1)
        packed = jnp.pad(packed, ((0, 1), (0, 0)))
        result.append((packed, jnp.pad(rank[:, 127], (0, 1), constant_values=1)))
    return result


def local(queries, keys, values, block_index, block_count, head_order):
    (kv_sent,) = split(split_kv_kernel, [(8, 2, 64, HD)], keys, values)
    kv_got = lax.all_to_all(kv_sent, ("zhi", "zlo"), split_axis=0, concat_axis=0, tiled=True)
    (q_sent,) = split(split_q_kernel, [(H, 64, HD)], queries)
    plan = tables(block_index, block_count)
    kv_got, q_sent, (ready, arriving) = lax.optimization_barrier((kv_got, q_sent, plan))
    low, high = kv_got[:4], kv_got[4:]
    low_next, high_next = partner(low, "x", 1), partner(high, "y", 1)
    q_own = lax.all_to_all(
        q_sent.reshape(4, GROUP * 64, HD), "zhi", split_axis=0, concat_axis=0, tiled=True
    ).reshape(TILES, 64, HD)
    q_oth = swap_cores(q_own)
    early, late = [], []
    for mine, other, inner, outer in ((low, low_next, "x", "y"), (high, high_next, "y", "x")):
        one = jnp.concatenate([mine, other])
        two = partner(one, inner, 3)
        one_next, two_next = partner(one, outer, 1), partner(two, outer, 3)
        early += [one, two, one_next, two_next]
        late += [
            partner(jnp.concatenate([one, one_next]), outer, 3),
            partner(jnp.concatenate([two, two_next]), outer, 1),
        ]
    *state, turned = attend(*ready, [q_own, q_oth], early, None)
    mine, others = attend(*arriving, [turned], late, state)
    attended = merge(mine, swap_cores(others))
    returned = lax.all_to_all(
        attended.reshape(4, GROUP * 64, HD), "zhi", split_axis=0, concat_axis=0, tiled=True
    ).reshape(H, 64, HD)
    return place(head_order, returned)


def solution(mesh):
    wide = Mesh(mesh.devices.reshape(4, 4, 4, 2, 2), AXES)
    tokens = P(AXES, None)
    return jax.shard_map(
        local,
        mesh=wide,
        in_specs=(tokens, tokens, tokens, P(), P(), P()),
        out_specs=tokens,
        check_vma=False,
    )
```

```python
import math
from functools import partial

import jax
import jax.numpy as jnp
from jax import lax
from jax.experimental import pallas as pl
from jax.experimental.pallas import tpu as pltpu
from jax.sharding import Mesh, PartitionSpec as P

H = 28
KVH = 4
HD = 128
BLOCK = 128
GROUP = H // KVH
TILES = 4 * GROUP
NB = 8
FLOOR = -1e30
EXP_SCALE = math.log2(math.e) / math.sqrt(HD)
AXES = ("zhi", "x", "y", "zlo", "core")


def partner(array, axis, mask):
    return lax.ppermute(array, axis, [(i, i ^ mask) for i in range(lax.axis_size(axis))])


def swap_cores(array):
    return partner(array, "core", 1)


def tree(op, parts):
    while len(parts) > 1:
        parts = [op(*parts[i:i + 2]) if i + 1 < len(parts) else parts[i] for i in range(0, len(parts), 2)]
    return parts[0]


def attend_kernel(first, pieces, *refs):
    refs = list(refs)
    take = lambda n: [refs.pop(0) for _ in range(n)]
    tab, cnt = take(2)
    queries = take(2) if first else take(1)
    sources = take(pieces)
    state_in = [] if first else take(3)
    outs = take(4) if first else take(2)
    (kv,) = take(1)
    s_bufs, m_bufs, a_bufs = take(4), take(4), take(4)
    m_ref, l_ref, acc = outs[:3] if first else take(3)
    qt = outs[3] if first else queries[0]
    lse, whole_out = (None, None) if first else take(2)
    (sem,) = refs
    core = lax.axis_index("core")
    unroll = 12 if first else 16
    started, at = [], 0
    for source in sources:
        started.append(pltpu.make_async_copy(source, kv.at[pl.ds(at, source.shape[0])], sem))
        at += source.shape[0]
    for copy in started:
        copy.start()

    def chunks_of(t):
        return jnp.maximum((cnt[t] + (NB - 1)) // NB, 1)

    total = lax.fori_loop(0, TILES, lambda t, n: n + chunks_of(t), jnp.int32(0))
    keys = lax.broadcasted_iota(jnp.int32, (64, BLOCK), 0)
    rows = lax.broadcasted_iota(jnp.int32, (64, BLOCK), 1)
    seen = (keys <= rows) & (rows < 64) | (rows >= 64) & (core == 0)

    def start(t, _):
        if first:
            qt[t] = jnp.concatenate([queries[0][t], queries[1][t]], axis=0).T
            m_ref[t] = jnp.full((8, BLOCK), FLOOR, jnp.float32)
            l_ref[t] = jnp.zeros((8, BLOCK), jnp.float32)
            acc[t] = jnp.zeros((HD, BLOCK), jnp.float32)
        else:
            m_ref[t], l_ref[t], acc[t] = (ref[t] for ref in state_in)
        return 0

    lax.fori_loop(0, TILES, start, 0, unroll=2)
    m_ref[TILES] = jnp.zeros((8, BLOCK), jnp.float32)
    l_ref[TILES] = jnp.zeros((8, BLOCK), jnp.float32)
    acc[TILES] = jnp.zeros((HD, BLOCK), jnp.float32)
    for copy in started:
        copy.wait()

    def block(t, c, j, which):
        return kv[tab[t, c * NB + j], which]

    def products(t, c, s_ref, m_buf, a_buf):
        k = jnp.concatenate([block(t, c, j, 0) for j in range(NB)], axis=0)
        s = jnp.dot(k, qt[jnp.minimum(t, TILES - 1)], preferred_element_type=jnp.float32)
        left_over = cnt[t] - c * NB
        d = jnp.minimum(left_over, NB) - 1
        tops = []
        for j in range(NB):
            part = s[j * 64:(j + 1) * 64]
            top = jnp.max(part.reshape(8, 8, BLOCK), axis=0)
            tops.append(jnp.where((left_over > j) & ((d != j) | (left_over > NB)) if first else left_over > j, top, FLOOR))
            cap = jnp.where(left_over > j, -FLOOR, FLOOR)
            s_ref[j * 64:(j + 1) * 64] = jnp.minimum(part, cap)
        if first:
            here = pl.ds(pl.multiple_of(d * 64, 64), 64)
            part = jnp.where(seen | (left_over > NB), s_ref[here, :], FLOOR)
            s_ref[here, :] = part
            tops.append(jnp.max(part.reshape(8, 8, BLOCK), axis=0))
        m_old = m_ref[t]
        m_new = jnp.maximum(m_old, jnp.max(tree(jnp.maximum, tops), axis=0, keepdims=True))
        m_ref[t] = m_new
        m_buf[...] = m_new
        a_buf[...] = jnp.exp2((m_old - m_new) * EXP_SCALE)

    def weigh(t, c, s_ref, m_buf, a_buf):
        m = m_buf[...][None]
        parts = []
        for j in range(NB):
            s = s_ref[j * 64:(j + 1) * 64].reshape(8, 8, BLOCK)
            parts.append(jnp.exp2((s - m) * EXP_SCALE).reshape(64, BLOCK))
        p = jnp.concatenate([part.astype(jnp.bfloat16) for part in parts], axis=0)
        part = tree(jnp.add, parts)
        part = tree(jnp.add, [part[i * 8:(i + 1) * 8] for i in range(8)])
        l_ref[t] = l_ref[t] * a_buf[...] + part
        v = jnp.concatenate([block(t, c, j, 1) for j in range(NB)], axis=0)
        update = lax.dot_general(
            v, p, (((0,), (0,)), ((), ())), preferred_element_type=jnp.float32
        )
        acc[t] = acc[t] * a_buf[:1] + update

    def steps(_, carry):
        items = list(carry)
        for k in range(unroll):
            t, c = items[0], items[1]
            old = (k - 3) % unroll
            products(t, c, s_bufs[k % 4], m_bufs[k % 4], a_bufs[k % 4])
            weigh(items[6], items[7], s_bufs[old % 4], m_bufs[old % 4], a_bufs[old % 4])
            last = c + 1 >= chunks_of(t)
            items = [
                jnp.where(last, jnp.minimum(t + 1, TILES), t),
                jnp.where(last, 0, c + 1),
            ] + items[:6]
        return tuple(items)

    zero, dummy = jnp.int32(0), jnp.int32(TILES)
    lax.fori_loop(0, (total + 2 + unroll) // unroll, steps, (zero, zero) + (dummy, zero) * 3)
    if first:
        return
    lse[...] = jnp.zeros_like(lse)

    def finish(t, _):
        whole = jnp.sum(l_ref[t], axis=0, keepdims=True)
        whole_out[t] = (acc[t] / whole).T
        lse[pl.ds(t, 1), :] = m_ref[t][:1] * EXP_SCALE + jnp.log2(whole)
        return 0

    leaving = []

    def leave(at, count):
        for i, out in enumerate(outs):
            leaving.append(
                pltpu.make_async_copy(
                    whole_out.at[pl.ds(at, count), pl.ds(i * 64, 64)],
                    out.at[pl.ds(at, count)],
                    sem,
                )
            )
            leaving[-1].start()

    for stripe in range(4):
        lax.fori_loop(stripe * GROUP, (stripe + 1) * GROUP, finish, 0, unroll=GROUP)
        leave(stripe * GROUP, GROUP)
    whole_out[TILES] = lse[...].T
    leave(TILES, 1)
    for copy in leaving:
        copy.wait()


def attend(tab, cnt, queries, pieces, state):
    vmem = pl.BlockSpec(memory_space=pltpu.VMEM)
    smem = pl.BlockSpec(memory_space=pltpu.SMEM)
    small = ((TILES + 1, 8, BLOCK), jnp.float32)
    large = ((TILES + 1, HD, BLOCK), jnp.float32)
    if state is None:
        shapes = [small, small, large, ((TILES, HD, BLOCK), jnp.bfloat16)]
        kept = []
    else:
        shapes = [((TILES + 1, 64, HD), jnp.float32)] * 2
        kept = [pltpu.VMEM(*small), pltpu.VMEM(*small), pltpu.VMEM(*large)]
        kept += [pltpu.VMEM((BLOCK, BLOCK), jnp.float32), pltpu.VMEM(*large)]
    slots = sum(piece.shape[0] for piece in pieces)
    flops = 2 * 2 * BLOCK * HD * 64 * TILES * slots // 2
    return pl.pallas_call(
        partial(attend_kernel, state is None, len(pieces)),
        out_shape=tuple(jax.ShapeDtypeStruct(*a) for a in shapes),
        in_specs=[smem, smem]
        + [vmem] * len(queries)
        + [pl.BlockSpec(memory_space=pl.ANY)] * len(pieces)
        + [vmem] * (0 if state is None else 3),
        out_specs=(vmem if state is None else pl.BlockSpec(memory_space=pltpu.HBM),) * len(shapes),
        scratch_shapes=[pltpu.VMEM((slots, 2, 64, HD), jnp.bfloat16)]
        + [pltpu.VMEM((NB * 64, BLOCK), jnp.float32)] * 4
        + [pltpu.VMEM((8, BLOCK), jnp.float32)] * 8
        + kept
        + [pltpu.SemaphoreType.DMA],
        compiler_params=pltpu.CompilerParams(vmem_limit_bytes=40 * 2**20),
        cost_estimate=pl.CostEstimate(
            flops=4 * flops, bytes_accessed=slots * 2**15, transcendentals=flops // 256
        ),
        name="attend",
    )(tab, cnt, *queries, *pieces, *(state or ()))


def merge_kernel(a_far, b_far, out_far, a, b, out, sems):
    spans = [(TILES, 1)] + [(i * GROUP, GROUP) for i in range(4)]
    arriving = [
        [
            pltpu.make_async_copy(
                far.at[pl.ds(at, count)], near.at[pl.ds(at, count)], sems.at[2 * i + k]
            )
            for k, (far, near) in enumerate(((a_far, a), (b_far, b)))
        ]
        for i, (at, count) in enumerate(spans)
    ]
    for copies in arriving:
        for copy in copies:
            copy.start()
    leaving = []
    for i, (at, count) in enumerate(spans):
        for copy in arriving[i]:
            copy.wait()
        if i == 0:
            top = jnp.maximum(a[TILES], b[TILES])
            w_a = jnp.exp2(a[TILES] - top)
            w_a = w_a / (w_a + jnp.exp2(b[TILES] - top))
            continue
        for t in range(at, at + count):
            out[t] = (b[t] + (a[t] - b[t]) * w_a[:, t:t + 1]).astype(jnp.bfloat16)
        leaving.append(
            pltpu.make_async_copy(
                out.at[pl.ds(at, count)], out_far.at[pl.ds(at, count)], sems.at[9 + i]
            )
        )
        leaving[-1].start()
    for copy in leaving:
        copy.wait()


def merge(a, b):
    far = pl.BlockSpec(memory_space=pltpu.HBM)
    part = pltpu.VMEM((TILES + 1, 64, HD), jnp.float32)
    return pl.pallas_call(
        merge_kernel,
        out_shape=jax.ShapeDtypeStruct((TILES, 64, HD), jnp.bfloat16),
        in_specs=[far, far],
        out_specs=far,
        scratch_shapes=[
            part, part, pltpu.VMEM((TILES, 64, HD), jnp.bfloat16), pltpu.SemaphoreType.DMA((14,))
        ],
        name="merge",
    )(a, b)


def place_kernel(spot, heads, out):
    for h in range(H):
        at = pl.multiple_of(spot[h] * HD, HD)
        out[:, pl.ds(at, HD)] = heads[h]


def place(order, heads):
    heads_iota = jnp.arange(H, dtype=jnp.int32)
    spot = jnp.sum(jnp.where(order[:, None] == heads_iota[None], heads_iota[:, None], 0), axis=0)
    return pl.pallas_call(
        place_kernel,
        out_shape=jax.ShapeDtypeStruct((64, H * HD), jnp.bfloat16),
        in_specs=[
            pl.BlockSpec(memory_space=pltpu.SMEM),
            pl.BlockSpec(memory_space=pltpu.VMEM),
        ],
        out_specs=pl.BlockSpec(memory_space=pltpu.VMEM),
        name="place",
    )(spot, heads)


def split_q_kernel(queries, out):
    for h in range(H):
        out[h] = queries[:, h * HD:(h + 1) * HD]


def split_kv_kernel(keys, values, out):
    for g in range(KVH):
        for copy in range(2):
            out[2 * g + copy, 0] = keys[:, g * HD:(g + 1) * HD]
            out[2 * g + copy, 1] = values[:, g * HD:(g + 1) * HD]


def split(kernel, shapes, *arrays):
    vmem = pl.BlockSpec(memory_space=pltpu.VMEM)
    return pl.pallas_call(
        kernel,
        out_shape=tuple(jax.ShapeDtypeStruct(shape, jnp.bfloat16) for shape in shapes),
        in_specs=[vmem] * len(arrays),
        out_specs=(vmem,) * len(shapes),
        name="split",
    )(*arrays)


def tables(block_index, block_count):
    here_x, here_y = lax.axis_index("x"), lax.axis_index("y")
    chip = (here_x * 4 + here_y) * 2 + lax.axis_index("zlo")
    group = lax.axis_index("zhi")
    index = block_index.reshape(4, 32, KVH, GROUP, 128)
    index = lax.dynamic_slice(index, (0, chip, group, 0, 0), (4, 1, 1, GROUP, 128))
    index = index.reshape(TILES, 128)
    count = block_count.reshape(4, 32, KVH, GROUP)
    count = lax.dynamic_slice(count, (0, chip, group, 0), (4, 1, 1, GROUP)).reshape(TILES, 1)

    z, inner = index // 32, index % 32
    rel_x, rel_y = (inner // 8) ^ here_x, (inner // 2 % 4) ^ here_y
    low = z < 2
    within, away = jnp.where(low, rel_x, rel_y), jnp.where(low, rel_y, rel_x)
    half = within // 2
    spot = jnp.where(half == 0, within, 3 - within) * 4 + z % 2 * 2 + inner % 2
    soon = away == jnp.where(half == 0, 1, 3)
    first = (away == 0) | soon
    slot_first = jnp.where(soon, 16, 0) + half * 8
    slot_second = half * 16 + jnp.where(away == 2, 8, 0)
    slot = jnp.where(first, slot_first, slot_second) + spot + jnp.where(low, 0, 32)
    entry = lax.broadcasted_iota(jnp.int32, (TILES, 128), 1)
    stage = jnp.where(entry < count, jnp.where(first, 0, 1), -1)
    before = lax.broadcasted_iota(jnp.int32, (128, 128), 0) <= lax.broadcasted_iota(
        jnp.int32, (128, 128), 1
    )
    result = []
    for number in range(2):
        member = stage == number
        rank = jnp.dot(
            member.astype(jnp.bfloat16), before.astype(jnp.bfloat16),
            preferred_element_type=jnp.float32,
        ).astype(jnp.int32)
        hit = (jnp.where(member, rank, 0)[:, :, None] - 1) == entry[:, None, :]
        packed = jnp.sum(jnp.where(hit, slot[:, :, None], 0), axis=1)
        packed = jnp.pad(packed, ((0, 1), (0, 0)))
        result.append((packed, jnp.pad(rank[:, 127], (0, 1), constant_values=1)))
    return result


def local(queries, keys, values, block_index, block_count, head_order):
    (kv_sent,) = split(split_kv_kernel, [(8, 2, 64, HD)], keys, values)
    kv_got = lax.all_to_all(kv_sent, ("zhi", "zlo"), split_axis=0, concat_axis=0, tiled=True)
    (q_sent,) = split(split_q_kernel, [(H, 64, HD)], queries)
    plan = tables(block_index, block_count)
    kv_got, q_sent, (ready, arriving) = lax.optimization_barrier((kv_got, q_sent, plan))
    low, high = kv_got[:4], kv_got[4:]
    low_next, high_next = partner(low, "x", 1), partner(high, "y", 1)
    q_own = lax.all_to_all(
        q_sent.reshape(4, GROUP * 64, HD), "zhi", split_axis=0, concat_axis=0, tiled=True
    ).reshape(TILES, 64, HD)
    q_oth = swap_cores(q_own)
    early, late = [], []
    for mine, other, inner, outer in ((low, low_next, "x", "y"), (high, high_next, "y", "x")):
        one = jnp.concatenate([mine, other])
        two = partner(one, inner, 3)
        one_next, two_next = partner(one, outer, 1), partner(two, outer, 3)
        early += [one, two, one_next, two_next]
        late += [
            partner(jnp.concatenate([one, one_next]), outer, 3),
            partner(jnp.concatenate([two, two_next]), outer, 1),
        ]
    *state, turned = attend(*ready, [q_own, q_oth], early, None)
    mine, others = attend(*arriving, [turned], late, state)
    attended = merge(mine, swap_cores(others))
    returned = lax.all_to_all(
        attended.reshape(4, GROUP * 64, HD), "zhi", split_axis=0, concat_axis=0, tiled=True
    ).reshape(H, 64, HD)
    return place(head_order, returned)


def solution(mesh):
    wide = Mesh(mesh.devices.reshape(4, 4, 4, 2, 2), AXES)
    tokens = P(AXES, None)
    return jax.shard_map(
        local,
        mesh=wide,
        in_specs=(tokens, tokens, tokens, P(), P(), P()),
        out_specs=tokens,
        check_vma=False,
    )
```

```python
import math
from functools import partial

import jax
import jax.numpy as jnp
from jax import lax
from jax.experimental import pallas as pl
from jax.experimental.pallas import tpu as pltpu
from jax.sharding import Mesh, PartitionSpec as P

H = 28
KVH = 4
HD = 128
BLOCK = 128
GROUP = H // KVH
TILES = 4 * GROUP
NB = 8
FLOOR = -1e30
EXP_SCALE = math.log2(math.e) / math.sqrt(HD)
AXES = ("zhi", "x", "y", "zlo", "core")


def partner(array, axis, mask):
    return lax.ppermute(array, axis, [(i, i ^ mask) for i in range(lax.axis_size(axis))])


def swap_cores(array):
    return partner(array, "core", 1)


def tree(op, parts):
    while len(parts) > 1:
        parts = [op(*parts[i:i + 2]) if i + 1 < len(parts) else parts[i] for i in range(0, len(parts), 2)]
    return parts[0]


def attend_kernel(first, pieces, *refs):
    refs = list(refs)
    take = lambda n: [refs.pop(0) for _ in range(n)]
    tab, cnt = take(2)
    queries = take(2) if first else take(1)
    sources = take(pieces)
    state_in = [] if first else take(3)
    outs = take(4) if first else take(2)
    (kv,) = take(1)
    s_bufs, m_bufs, a_bufs = take(4), take(4), take(4)
    m_ref, l_ref, acc = outs[:3] if first else take(3)
    qt = outs[3] if first else queries[0]
    lse, whole_out = (None, None) if first else take(2)
    (sem,) = refs
    core = lax.axis_index("core")
    unroll = 12 if first else 16
    started, at = [], 0
    for source in sources:
        started.append(pltpu.make_async_copy(source, kv.at[pl.ds(at, source.shape[0])], sem))
        at += source.shape[0]
    for copy in started:
        copy.start()

    def chunks_of(t):
        return jnp.maximum((cnt[t] + (NB - 1)) // NB, 1)

    total = lax.fori_loop(0, TILES, lambda t, n: n + chunks_of(t), jnp.int32(0))
    keys = lax.broadcasted_iota(jnp.int32, (64, BLOCK), 0)
    rows = lax.broadcasted_iota(jnp.int32, (64, BLOCK), 1)
    seen = (keys <= rows) & (rows < 64) | (rows >= 64) & (core == 0)

    def start(t, _):
        if first:
            qt[t] = jnp.concatenate([queries[0][t], queries[1][t]], axis=0).T
            m_ref[t] = jnp.full((8, BLOCK), FLOOR, jnp.float32)
            l_ref[t] = jnp.zeros((8, BLOCK), jnp.float32)
            acc[t] = jnp.zeros((HD, BLOCK), jnp.float32)
        else:
            m_ref[t], l_ref[t], acc[t] = (ref[t] for ref in state_in)
        return 0

    lax.fori_loop(0, TILES, start, 0, unroll=2)
    m_ref[TILES] = jnp.zeros((8, BLOCK), jnp.float32)
    l_ref[TILES] = jnp.zeros((8, BLOCK), jnp.float32)
    acc[TILES] = jnp.zeros((HD, BLOCK), jnp.float32)
    for copy in started:
        copy.wait()

    def block(t, c, j, which):
        return kv[tab[t, c * NB + j], which]

    def products(t, c, s_ref, m_buf, a_buf):
        k = jnp.concatenate([block(t, c, j, 0) for j in range(NB)], axis=0)
        s = jnp.dot(k, qt[jnp.minimum(t, TILES - 1)], preferred_element_type=jnp.float32)
        left_over = cnt[t] - c * NB
        d = jnp.minimum(left_over, NB) - 1
        tops = []
        for j in range(NB):
            part = s[j * 64:(j + 1) * 64]
            top = jnp.max(part.reshape(8, 8, BLOCK), axis=0)
            tops.append(jnp.where((left_over > j) & ((d != j) | (left_over > NB)) if first else left_over > j, top, FLOOR))
            cap = jnp.where(left_over > j, -FLOOR, FLOOR)
            s_ref[j * 64:(j + 1) * 64] = jnp.minimum(part, cap)
        if first:
            here = pl.ds(pl.multiple_of(d * 64, 64), 64)
            part = jnp.where(seen | (left_over > NB), s_ref[here, :], FLOOR)
            s_ref[here, :] = part
            tops.append(jnp.max(part.reshape(8, 8, BLOCK), axis=0))
        m_old = m_ref[t]
        m_new = jnp.maximum(m_old, jnp.max(tree(jnp.maximum, tops), axis=0, keepdims=True))
        m_ref[t] = m_new
        m_buf[...] = m_new
        a_buf[...] = jnp.exp2((m_old - m_new) * EXP_SCALE)

    def weigh(t, c, s_ref, m_buf, a_buf):
        m = m_buf[...][None]
        parts = []
        for j in range(NB):
            s = s_ref[j * 64:(j + 1) * 64].reshape(8, 8, BLOCK)
            parts.append(jnp.exp2((s - m) * EXP_SCALE).reshape(64, BLOCK))
        p = jnp.concatenate([part.astype(jnp.bfloat16) for part in parts], axis=0)
        part = tree(jnp.add, parts)
        part = tree(jnp.add, [part[i * 8:(i + 1) * 8] for i in range(8)])
        l_ref[t] = l_ref[t] * a_buf[...] + part
        v = jnp.concatenate([block(t, c, j, 1) for j in range(NB)], axis=0)
        update = lax.dot_general(
            v, p, (((0,), (0,)), ((), ())), preferred_element_type=jnp.float32
        )
        acc[t] = acc[t] * a_buf[:1] + update

    def steps(_, carry):
        items = list(carry)
        for k in range(unroll):
            t, c = items[0], items[1]
            old = (k - 3) % unroll
            products(t, c, s_bufs[k % 4], m_bufs[k % 4], a_bufs[k % 4])
            weigh(items[6], items[7], s_bufs[old % 4], m_bufs[old % 4], a_bufs[old % 4])
            last = c + 1 >= chunks_of(t)
            items = [
                jnp.where(last, jnp.minimum(t + 1, TILES), t),
                jnp.where(last, 0, c + 1),
            ] + items[:6]
        return tuple(items)

    zero, dummy = jnp.int32(0), jnp.int32(TILES)
    lax.fori_loop(0, (total + 2 + unroll) // unroll, steps, (zero, zero) + (dummy, zero) * 3)
    if first:
        return
    lse[...] = jnp.zeros_like(lse)

    def finish(t):
        whole = jnp.sum(l_ref[t], axis=0, keepdims=True)
        whole_out[t] = (acc[t] * (1.0 / whole)).T
        lse[t:t + 1, :] = m_ref[t, :1] * EXP_SCALE + jnp.log2(whole)

    leaving = []

    def leave(at, count):
        for i, out in enumerate(outs):
            leaving.append(
                pltpu.make_async_copy(
                    whole_out.at[pl.ds(at, count), pl.ds(i * 64, 64)],
                    out.at[pl.ds(at, count)],
                    sem,
                )
            )
            leaving[-1].start()

    for stripe in range(4):
        for t in range(stripe * GROUP, (stripe + 1) * GROUP):
            finish(t)
        leave(stripe * GROUP, GROUP)
    whole_out[TILES] = lse[...].T
    leave(TILES, 1)
    for copy in leaving:
        copy.wait()


def attend(tab, cnt, queries, pieces, state):
    vmem = pl.BlockSpec(memory_space=pltpu.VMEM)
    smem = pl.BlockSpec(memory_space=pltpu.SMEM)
    small = ((TILES + 1, 8, BLOCK), jnp.float32)
    large = ((TILES + 1, HD, BLOCK), jnp.float32)
    if state is None:
        shapes = [small, small, large, ((TILES, HD, BLOCK), jnp.bfloat16)]
        kept = []
    else:
        shapes = [((TILES + 1, 64, HD), jnp.float32)] * 2
        kept = [pltpu.VMEM(*small), pltpu.VMEM(*small), pltpu.VMEM(*large)]
        kept += [pltpu.VMEM((BLOCK, BLOCK), jnp.float32), pltpu.VMEM(*large)]
    slots = sum(piece.shape[0] for piece in pieces)
    flops = 2 * 2 * BLOCK * HD * 64 * TILES * slots // 2
    return pl.pallas_call(
        partial(attend_kernel, state is None, len(pieces)),
        out_shape=tuple(jax.ShapeDtypeStruct(*a) for a in shapes),
        in_specs=[smem, smem]
        + [vmem] * len(queries)
        + [pl.BlockSpec(memory_space=pl.ANY)] * len(pieces)
        + [vmem] * (0 if state is None else 3),
        out_specs=(vmem if state is None else pl.BlockSpec(memory_space=pltpu.HBM),) * len(shapes),
        scratch_shapes=[pltpu.VMEM((slots, 2, 64, HD), jnp.bfloat16)]
        + [pltpu.VMEM((NB * 64, BLOCK), jnp.float32)] * 4
        + [pltpu.VMEM((8, BLOCK), jnp.float32)] * 8
        + kept
        + [pltpu.SemaphoreType.DMA],
        compiler_params=pltpu.CompilerParams(vmem_limit_bytes=40 * 2**20),
        cost_estimate=pl.CostEstimate(
            flops=4 * flops, bytes_accessed=slots * 2**15, transcendentals=flops // 256
        ),
        name="attend",
    )(tab, cnt, *queries, *pieces, *(state or ()))


def merge_kernel(a_far, b_far, out_far, a, b, out, sems):
    spans = [(TILES, 1)] + [(i * GROUP, GROUP) for i in range(4)]
    arriving = [
        [
            pltpu.make_async_copy(
                far.at[pl.ds(at, count)], near.at[pl.ds(at, count)], sems.at[2 * i + k]
            )
            for k, (far, near) in enumerate(((a_far, a), (b_far, b)))
        ]
        for i, (at, count) in enumerate(spans)
    ]
    for copies in arriving:
        for copy in copies:
            copy.start()
    leaving = []
    for i, (at, count) in enumerate(spans):
        for copy in arriving[i]:
            copy.wait()
        if i == 0:
            top = jnp.maximum(a[TILES], b[TILES])
            w_a = jnp.exp2(a[TILES] - top)
            w_a = w_a / (w_a + jnp.exp2(b[TILES] - top))
            continue
        for t in range(at, at + count):
            out[t] = (b[t] + (a[t] - b[t]) * w_a[:, t:t + 1]).astype(jnp.bfloat16)
        leaving.append(
            pltpu.make_async_copy(
                out.at[pl.ds(at, count)], out_far.at[pl.ds(at, count)], sems.at[9 + i]
            )
        )
        leaving[-1].start()
    for copy in leaving:
        copy.wait()


def merge(a, b):
    far = pl.BlockSpec(memory_space=pltpu.HBM)
    part = pltpu.VMEM((TILES + 1, 64, HD), jnp.float32)
    return pl.pallas_call(
        merge_kernel,
        out_shape=jax.ShapeDtypeStruct((TILES, 64, HD), jnp.bfloat16),
        in_specs=[far, far],
        out_specs=far,
        scratch_shapes=[
            part, part, pltpu.VMEM((TILES, 64, HD), jnp.bfloat16), pltpu.SemaphoreType.DMA((14,))
        ],
        name="merge",
    )(a, b)


def place_kernel(spot, heads, out):
    for h in range(H):
        at = pl.multiple_of(spot[h] * HD, HD)
        out[:, pl.ds(at, HD)] = heads[h]


def place(order, heads):
    heads_iota = jnp.arange(H, dtype=jnp.int32)
    spot = jnp.sum(jnp.where(order[:, None] == heads_iota[None], heads_iota[:, None], 0), axis=0)
    return pl.pallas_call(
        place_kernel,
        out_shape=jax.ShapeDtypeStruct((64, H * HD), jnp.bfloat16),
        in_specs=[
            pl.BlockSpec(memory_space=pltpu.SMEM),
            pl.BlockSpec(memory_space=pltpu.VMEM),
        ],
        out_specs=pl.BlockSpec(memory_space=pltpu.VMEM),
        name="place",
    )(spot, heads)


def split_q_kernel(queries, out):
    for h in range(H):
        out[h] = queries[:, h * HD:(h + 1) * HD]


def split_kv_kernel(keys, values, out):
    for g in range(KVH):
        for copy in range(2):
            out[2 * g + copy, 0] = keys[:, g * HD:(g + 1) * HD]
            out[2 * g + copy, 1] = values[:, g * HD:(g + 1) * HD]


def split(kernel, shapes, *arrays):
    vmem = pl.BlockSpec(memory_space=pltpu.VMEM)
    return pl.pallas_call(
        kernel,
        out_shape=tuple(jax.ShapeDtypeStruct(shape, jnp.bfloat16) for shape in shapes),
        in_specs=[vmem] * len(arrays),
        out_specs=(vmem,) * len(shapes),
        name="split",
    )(*arrays)


def tables(block_index, block_count):
    here_x, here_y = lax.axis_index("x"), lax.axis_index("y")
    chip = (here_x * 4 + here_y) * 2 + lax.axis_index("zlo")
    group = lax.axis_index("zhi")
    index = block_index.reshape(4, 32, KVH, GROUP, 128)
    index = lax.dynamic_slice(index, (0, chip, group, 0, 0), (4, 1, 1, GROUP, 128))
    index = index.reshape(TILES, 128)
    count = block_count.reshape(4, 32, KVH, GROUP)
    count = lax.dynamic_slice(count, (0, chip, group, 0), (4, 1, 1, GROUP)).reshape(TILES, 1)

    z, inner = index // 32, index % 32
    rel_x, rel_y = (inner // 8) ^ here_x, (inner // 2 % 4) ^ here_y
    low = z < 2
    within, away = jnp.where(low, rel_x, rel_y), jnp.where(low, rel_y, rel_x)
    half = within // 2
    spot = jnp.where(half == 0, within, 3 - within) * 4 + z % 2 * 2 + inner % 2
    soon = away == jnp.where(half == 0, 1, 3)
    first = (away == 0) | soon
    slot_first = jnp.where(soon, 16, 0) + half * 8
    slot_second = half * 16 + jnp.where(away == 2, 8, 0)
    slot = jnp.where(first, slot_first, slot_second) + spot + jnp.where(low, 0, 32)
    entry = lax.broadcasted_iota(jnp.int32, (TILES, 128), 1)
    stage = jnp.where(entry < count, jnp.where(first, 0, 1), -1)
    before = lax.broadcasted_iota(jnp.int32, (128, 128), 0) <= lax.broadcasted_iota(
        jnp.int32, (128, 128), 1
    )
    result = []
    for number in range(2):
        member = stage == number
        rank = jnp.dot(
            member.astype(jnp.bfloat16), before.astype(jnp.bfloat16),
            preferred_element_type=jnp.float32,
        ).astype(jnp.int32)
        hit = (jnp.where(member, rank, 0)[:, :, None] - 1) == entry[:, None, :]
        packed = jnp.sum(jnp.where(hit, slot[:, :, None], 0), axis=1)
        packed = jnp.pad(packed, ((0, 1), (0, 0)))
        result.append((packed, jnp.pad(rank[:, 127], (0, 1), constant_values=1)))
    return result


def local(queries, keys, values, block_index, block_count, head_order):
    (kv_sent,) = split(split_kv_kernel, [(8, 2, 64, HD)], keys, values)
    kv_got = lax.all_to_all(kv_sent, ("zhi", "zlo"), split_axis=0, concat_axis=0, tiled=True)
    (q_sent,) = split(split_q_kernel, [(H, 64, HD)], queries)
    plan = tables(block_index, block_count)
    kv_got, q_sent, (ready, arriving) = lax.optimization_barrier((kv_got, q_sent, plan))
    low, high = kv_got[:4], kv_got[4:]
    low_next, high_next = partner(low, "x", 1), partner(high, "y", 1)
    q_own = lax.all_to_all(
        q_sent.reshape(4, GROUP * 64, HD), "zhi", split_axis=0, concat_axis=0, tiled=True
    ).reshape(TILES, 64, HD)
    q_oth = swap_cores(q_own)
    early, late = [], []
    for mine, other, inner, outer in ((low, low_next, "x", "y"), (high, high_next, "y", "x")):
        one = jnp.concatenate([mine, other])
        two = partner(one, inner, 3)
        one_next, two_next = partner(one, outer, 1), partner(two, outer, 3)
        early += [one, two, one_next, two_next]
        late += [
            partner(jnp.concatenate([one, one_next]), outer, 3),
            partner(jnp.concatenate([two, two_next]), outer, 1),
        ]
    *state, turned = attend(*ready, [q_own, q_oth], early, None)
    mine, others = attend(*arriving, [turned], late, state)
    attended = merge(mine, swap_cores(others))
    returned = lax.all_to_all(
        attended.reshape(4, GROUP * 64, HD), "zhi", split_axis=0, concat_axis=0, tiled=True
    ).reshape(H, 64, HD)
    return place(head_order, returned)


def solution(mesh):
    wide = Mesh(mesh.devices.reshape(4, 4, 4, 2, 2), AXES)
    tokens = P(AXES, None)
    return jax.shard_map(
        local,
        mesh=wide,
        in_specs=(tokens, tokens, tokens, P(), P(), P()),
        out_specs=tokens,
        check_vma=False,
    )
```
